32 devices in a mesh: row: 8 (over z, core), col: 4 (over y, x).
Axes of the slice: x: 2, y: 2, z: 4, core: 2. Of those that a mesh axis runs over, the one named last changes fastest.
Arguments:
- queries: bfloat16 [1024, 2048], P('row'), may hold values from -18 to 18
- keys: bfloat16 [1024, 1024], P(('row', 'col')), may hold values from -6 to 6
- values: bfloat16 [1024, 1024], P(('row', 'col')), may hold values from -6 to 6
Outputs:
- attended: bfloat16 [1024, 2048], P(('row', 'col'))
The draws below stay inside these ranges and needn't reach their ends.
All inputs are finite; a program needn't handle non-finite values.
Results may differ from the reference program's by a relative error of at most 0.0095.
Values may be sent and summed in bfloat16 or wider, within the bound.
No kernel may reach another device: no remote copies, remote signals or barrier semaphores. Data moves between devices by JAX's collectives and lax.ppermute only.
A program may use at most 64 MiB of HBM per device.

```python
import jax
import jax.numpy as jnp
from jax import lax

QUERY_HEADS = 8
KEY_VALUE_HEADS = 4
HEAD_SIZE = 256
BLOCK_POSITIONS = 32
SEQUENCE_LENGTH = 1024
N_ROW = 8
N_COL = 4


def steps_of(key, extent, cuts, low, largest):
    loudness = 1.0
    for position, parts in cuts:
        draws = jax.random.uniform(jax.random.fold_in(jax.random.fold_in(key, 6), position), (parts,), jnp.float32, low / len(cuts), largest / len(cuts))
        loudness = loudness * jnp.repeat(jnp.exp(draws), extent[position] // parts).reshape((-1,) + (1,) * (len(extent) - 1 - position))
    return loudness


def scatter_about(rng, extent, width, limit, pieces=(), held_as=jnp.bfloat16):
    entries = width * jax.random.normal(rng, extent, jnp.float32)
    if pieces:
        entries = entries * steps_of(rng, extent, pieces, -0.22, 0.18)
    return jnp.clip(entries, -limit, limit).astype(held_as)


def setup_inputs(seed: int = 0) -> dict:
    splits = jax.random.split(jax.random.key(seed), 4)
    queries = scatter_about(splits[0], (SEQUENCE_LENGTH, QUERY_HEADS * HEAD_SIZE), 3.0, 18.0, ((0, 8),))
    keys = scatter_about(splits[1], (SEQUENCE_LENGTH, KEY_VALUE_HEADS * HEAD_SIZE), 1.0, 6.0, ((0, 32),))
    values = scatter_about(splits[2], (SEQUENCE_LENGTH, KEY_VALUE_HEADS * HEAD_SIZE), 1.0, 6.0, ((0, 32),))
    return {"queries": queries, "keys": keys, "values": values}


SCALE = 0.0625
CAP = 50.0


def reference(queries, keys, values):
    length_total = BLOCK_POSITIONS * N_ROW * N_COL
    block_slice = min(512, length_total)
    head_group = QUERY_HEADS // KEY_VALUE_HEADS
    key_float = keys.astype(jnp.float32).reshape(length_total, KEY_VALUE_HEADS, HEAD_SIZE)
    value_portion = values.astype(jnp.float32).reshape(N_ROW, N_COL, BLOCK_POSITIONS, KEY_VALUE_HEADS, HEAD_SIZE)
    key_pos = jnp.arange(length_total, dtype=jnp.int32)

    def one_block(index):
        start = (index * block_slice).astype(jnp.int32)
        query_block = lax.dynamic_slice_in_dim(queries, start, block_slice, 0)
        query_float = query_block.astype(jnp.float32).reshape(block_slice, KEY_VALUE_HEADS, head_group, HEAD_SIZE)
        scores = jnp.einsum("qkgd,nkd->kgqn", query_float, key_float) * SCALE
        capped = CAP * jnp.tanh(scores / CAP)
        query_pos = start + jnp.arange(block_slice, dtype=jnp.int32)
        allowed = key_pos[None, :] <= query_pos[:, None]
        weights = jnp.where(allowed[None, None], jnp.exp(capped), jnp.float32(0.0))
        denominator = jnp.sum(weights, axis=-1)
        rounded_length = lax.optimization_barrier(weights.astype(jnp.bfloat16)).astype(jnp.float32)
        rounded_length = rounded_length.reshape(KEY_VALUE_HEADS, head_group, block_slice, N_ROW, N_COL, BLOCK_POSITIONS)
        partial_f = jnp.einsum("kgqrcb,rcbkd->cqkgd", rounded_length, value_portion)
        partial_r = lax.optimization_barrier(partial_f.astype(jnp.bfloat16)).astype(jnp.float32)
        numerator = jnp.sum(partial_r, axis=0).reshape(block_slice, QUERY_HEADS, HEAD_SIZE)
        denom_rows = jnp.transpose(denominator, (2, 0, 1)).reshape(block_slice, QUERY_HEADS)
        return (numerator / denom_rows[:, :, None]).reshape(block_slice, QUERY_HEADS * HEAD_SIZE).astype(jnp.bfloat16)

    outputs = lax.map(one_block, jnp.arange(length_total // block_slice, dtype=jnp.int32))
    return outputs.reshape(length_total, QUERY_HEADS * HEAD_SIZE)
```

```python
import math

import jax
import jax.numpy as jnp
from jax import lax
from jax.experimental import pallas as pl
from jax.experimental.pallas import tpu as pltpu
from jax.sharding import PartitionSpec as P

HEAD = 256
SCALE = 0.0625
CAP = 50.0
LANES = 128


def attend_kernel(order, blk, n_col, q_ref, *refs):
    n_src = len(order)
    srcs, outs = refs[:n_src], refs[n_src : n_src + n_col]
    k_all, v_all = refs[n_src + n_col :]
    row, col = lax.axis_index("row"), lax.axis_index("col")
    feat_q, feat_k = q_ref.shape[1], srcs[0].shape[1]
    kv_heads = feat_k // HEAD
    group = feat_q // feat_k
    span = n_col * blk
    n_keys = n_src * blk
    for t, src in enumerate(srcs):
        k_all[t * blk : (t + 1) * blk, :] = src[:blk, :]
        v_all[t * blk : (t + 1) * blk, :] = src[blk:, :]
    lane = lax.broadcasted_iota(jnp.int32, (1, n_keys), 1)
    key_pos = jnp.zeros((1, n_keys), jnp.int32)
    for t, mask in enumerate(order):
        start = ((row ^ mask) * n_col + col) * blk
        key_pos = jnp.where(lane // blk == t, start + lane % blk, key_pos)
    chunk = min(n_col, 4)
    for base in range(0, n_col, chunk):
        parts = [pl.ds(pl.multiple_of((col ^ j) * blk, blk), blk) for j in range(base, base + chunk)]
        sub = lax.broadcasted_iota(jnp.int32, (blk, 1), 0)
        pos = jnp.concatenate(
            [row * span + (col ^ j) * blk + sub for j in range(base, base + chunk)], axis=0
        )
        rows = chunk * blk
        keep = jnp.where(key_pos <= pos, 1.0, 0.0).astype(jnp.float32)
        tail_lane = lax.broadcasted_iota(jnp.int32, (rows, LANES), 1)
        high = jnp.zeros((rows, LANES), jnp.float32)
        low = jnp.zeros((rows, LANES), jnp.float32)
        for kv in range(kv_heads):
            k_head = k_all[:, kv * HEAD : (kv + 1) * HEAD]
            v_head = v_all[:, kv * HEAD : (kv + 1) * HEAD]
            for g in range(group):
                h = kv * group + g
                q_head = jnp.concatenate(
                    [q_ref[part, h * HEAD : (h + 1) * HEAD] for part in parts], axis=0
                )
                scores = lax.dot_general(
                    q_head, k_head, (((1,), (1,)), ((), ())), preferred_element_type=jnp.float32
                )
                capped = jnp.tanh(scores * (SCALE / CAP)) * (CAP / math.log(2.0))
                weights = jnp.exp2(capped) * keep
                denom = jnp.sum(weights, axis=1, keepdims=True)
                numer = jnp.dot(
                    weights.astype(jnp.bfloat16), v_head, preferred_element_type=jnp.float32
                ).astype(jnp.bfloat16)
                for i in range(chunk):
                    outs[base + i][:, h * HEAD : (h + 1) * HEAD] = numer[i * blk : (i + 1) * blk]
                rounded = denom.astype(jnp.bfloat16).astype(jnp.float32)
                high = jnp.where(tail_lane == h, rounded, high)
                low = jnp.where(tail_lane == h, denom - rounded, low)
        for i in range(chunk):
            part = slice(i * blk, (i + 1) * blk)
            outs[base + i][:, feat_q : feat_q + LANES] = high[part].astype(jnp.bfloat16)
            outs[base + i][:, feat_q + LANES :] = low[part].astype(jnp.bfloat16)


def combine_kernel(*refs):
    parts, out_ref = refs[:-1], refs[-1]
    feat_q = out_ref.shape[1]
    tail = sum(p[:, feat_q:].astype(jnp.float32) for p in parts)
    denom = tail[:, :LANES] + tail[:, LANES:]
    for h in range(feat_q // HEAD):
        cut = slice(h * HEAD, (h + 1) * HEAD)
        numer = sum(p[:, cut].astype(jnp.float32) for p in parts)
        out_ref[:, cut] = (numer / denom[:, h : h + 1]).astype(jnp.bfloat16)


def per_device(queries, keys, values):
    blk, feat_k = keys.shape
    feat_q = queries.shape[1]
    n_row = lax.axis_size("row")
    n_col = lax.axis_size("col")

    def swap_row(x, mask):
        return lax.ppermute(x, "row", [(i, i ^ mask) for i in range(n_row)])

    def swap_col(x, mask):
        return lax.ppermute(x, "col", [(i, i ^ mask) for i in range(n_col)])

    own = jnp.concatenate([keys, values], axis=0)
    blocks = {0: own}
    for mask in range(2, n_row, 2):
        blocks[mask] = swap_row(own, mask)
    for mask in range(0, n_row, 2):
        blocks[mask ^ 1] = swap_row(blocks[mask], 1)
    order = sorted(blocks)
    n_keys = n_row * blk
    vmem = pl.BlockSpec(memory_space=pltpu.VMEM)
    wide = feat_q + 2 * LANES
    messages = pl.pallas_call(
        lambda *refs: attend_kernel(order, blk, n_col, *refs),
        out_shape=[jax.ShapeDtypeStruct((blk, wide), jnp.bfloat16)] * n_col,
        in_specs=[vmem] * (1 + n_row),
        out_specs=[vmem] * n_col,
        scratch_shapes=[
            pltpu.VMEM((n_keys, feat_k), jnp.bfloat16),
            pltpu.VMEM((n_keys, feat_k), jnp.bfloat16),
        ],
        compiler_params=pltpu.CompilerParams(vmem_limit_bytes=40 * 2**20),
        name="attend",
    )(queries, *[blocks[m] for m in order])
    received = [messages[0]] + [swap_col(messages[j], j) for j in range(1, n_col)]
    return pl.pallas_call(
        combine_kernel,
        out_shape=jax.ShapeDtypeStruct((blk, feat_q), jnp.bfloat16),
        in_specs=[vmem] * n_col,
        out_specs=vmem,
        name="combine",
    )(*received)


def solution(mesh):
    return jax.shard_map(
        per_device,
        mesh=mesh,
        in_specs=(P("row", None), P(("row", "col"), None), P(("row", "col"), None)),
        out_specs=P(("row", "col"), None),
        check_vma=False,
    )
```

```python
import functools
import math

import jax
import jax.numpy as jnp
from jax import lax
from jax.experimental import pallas as pl
from jax.experimental.pallas import tpu as pltpu
from jax.sharding import PartitionSpec as P

HEAD = 256
SCALE = 0.0625
CAP = 50.0
LANES = 128
VMEM = pl.BlockSpec(memory_space=pltpu.VMEM)


def stack_blocks(srcs, k_all, v_all, blk):
    for t, src in enumerate(srcs):
        k_all[t * blk : (t + 1) * blk, :] = src[:blk, :]
        v_all[t * blk : (t + 1) * blk, :] = src[blk:, :]


def group_sums(masks, blk, n_col, dests, q_ref, k_all, v_all, emit):
    row, col = lax.axis_index("row"), lax.axis_index("col")
    kv_heads = k_all.shape[1] // HEAD
    group = q_ref.shape[1] // k_all.shape[1]
    n_keys = len(masks) * blk
    lane = lax.broadcasted_iota(jnp.int32, (1, n_keys), 1)
    key_pos = jnp.zeros((1, n_keys), jnp.int32)
    for t, mask in enumerate(masks):
        start = ((row ^ mask) * n_col + col) * blk
        key_pos = jnp.where(lane // blk == t, start + lane % blk, key_pos)
    sub = lax.broadcasted_iota(jnp.int32, (blk, 1), 0)
    parts = [pl.ds(pl.multiple_of((col ^ d) * blk, blk), blk) for d in dests]
    pos = jnp.concatenate([(row * n_col + (col ^ d)) * blk + sub for d in dests], axis=0)
    keep = jnp.where(key_pos <= pos, 1.0, 0.0).astype(jnp.float32)
    for kv in range(kv_heads):
        k_head = k_all[:, kv * HEAD : (kv + 1) * HEAD]
        v_head = v_all[:, kv * HEAD : (kv + 1) * HEAD]
        for h in range(kv * group, (kv + 1) * group):
            q_head = jnp.concatenate([q_ref[p, h * HEAD : (h + 1) * HEAD] for p in parts], axis=0)
            scores = lax.dot_general(
                q_head, k_head, (((1,), (1,)), ((), ())), preferred_element_type=jnp.float32
            )
            capped = jnp.tanh(scores * (SCALE / CAP)) * (CAP / math.log(2.0))
            weights = jnp.exp2(capped) * keep
            denom = jnp.sum(weights, axis=1, keepdims=True)
            numer = jnp.dot(
                weights.astype(jnp.bfloat16), v_head, preferred_element_type=jnp.float32
            )
            emit(h, numer, denom)


def chunks_of(n_col):
    size = min(n_col, 4)
    return [range(base, base + size) for base in range(0, n_col, size)]


def sums_kernel(masks, sums_in, last, blk, n_col, q_ref, *refs):
    before, refs = refs[: 2 * sums_in], refs[2 * sums_in :]
    n_src = len(masks)
    srcs, outs, (k_all, v_all) = refs[:n_src], refs[n_src:-2], refs[-2:]
    feat_q = q_ref.shape[1]
    stack_blocks(srcs, k_all, v_all, blk)
    for dests in chunks_of(n_col):
        rows = slice(dests[0] * blk, (dests[-1] + 1) * blk)
        lanes = lax.broadcasted_iota(jnp.int32, (len(dests) * blk, LANES), 1)
        total = [before[1][rows, :] if sums_in else jnp.zeros(lanes.shape, jnp.float32)]

        def emit(h, numer, denom, dests=dests, rows=rows, lanes=lanes, total=total):
            cut = slice(h * HEAD, (h + 1) * HEAD)
            if sums_in:
                numer = numer + before[0][rows, cut]
            if last:
                numer = numer.astype(jnp.bfloat16)
                for i, d in enumerate(dests):
                    outs[d][:, cut] = numer[i * blk : (i + 1) * blk]
            else:
                outs[0][rows, cut] = numer
            total[0] = total[0] + jnp.where(lanes % (LANES // 2) == h, denom, 0.0)

        group_sums(masks, blk, n_col, dests, q_ref, k_all, v_all, emit)
        if last:
            high = total[0].astype(jnp.bfloat16).astype(jnp.float32)
            tail = jnp.where(lanes < LANES // 2, high, total[0] - high).astype(jnp.bfloat16)
            for i, d in enumerate(dests):
                outs[d][:, feat_q:] = tail[i * blk : (i + 1) * blk]
        else:
            outs[1][rows, :] = total[0]


def combine_kernel(*refs):
    parts, out_ref = refs[:-1], refs[-1]
    feat_q = out_ref.shape[1]
    tail = sum(p[:, feat_q:].astype(jnp.float32) for p in parts)
    inverse = 1.0 / (tail + pltpu.roll(tail, LANES // 2, 1))
    for h in range(feat_q // HEAD):
        cut = slice(h * HEAD, (h + 1) * HEAD)
        numer = sum(p[:, cut].astype(jnp.float32) for p in parts)
        out_ref[:, cut] = (numer * inverse[:, h : h + 1]).astype(jnp.bfloat16)


def per_device(queries, keys, values):
    blk, feat_k = keys.shape
    span, feat_q = queries.shape
    n_row = lax.axis_size("row")
    n_col = lax.axis_size("col")

    def swap_row(x, mask):
        return lax.ppermute(x, "row", [(i, i ^ mask) for i in range(n_row)])

    def swap_col(x, mask):
        return lax.ppermute(x, "col", [(i, i ^ mask) for i in range(n_col)])

    def sums(masks, before, last, name):
        message = jax.ShapeDtypeStruct((blk, feat_q + LANES), jnp.bfloat16)
        totals = [
            jax.ShapeDtypeStruct((span, feat_q), jnp.float32),
            jax.ShapeDtypeStruct((span, LANES), jnp.float32),
        ]
        out_shape = [message] * n_col if last else totals
        args = [queries, *before, *[blocks[m] for m in masks]]
        return pl.pallas_call(
            functools.partial(sums_kernel, masks, len(before) // 2, last, blk, n_col),
            out_shape=out_shape,
            in_specs=[VMEM] * len(args),
            out_specs=[VMEM] * len(out_shape),
            scratch_shapes=[pltpu.VMEM((len(masks) * blk, feat_k), jnp.bfloat16)] * 2,
            compiler_params=pltpu.CompilerParams(vmem_limit_bytes=limit),
            name=name,
        )(*args)

    limit = 16 * 2**20 if span * n_row <= 4096 else 40 * 2**20
    own = jnp.concatenate([keys, values], axis=0)
    blocks = {0: own, 1: swap_row(own, 1)}
    far = list(range(2, n_row, 2))
    for mask in far:
        blocks[mask] = swap_row(own, mask)
    totals = sums([0, 1], [], False, "own_chip")
    *totals, arrived = lax.optimization_barrier((*totals, [blocks[m] for m in far]))
    blocks.update(zip(far, arrived))
    for mask in far:
        blocks[mask ^ 1] = swap_row(blocks[mask], 1)
    totals = sums(far, totals, False, "far_same_core")
    messages = sums([m ^ 1 for m in far], totals, True, "far_other_core")
    received = [messages[0]] + [swap_col(messages[j], j) for j in range(1, n_col)]
    return pl.pallas_call(
        combine_kernel,
        out_shape=jax.ShapeDtypeStruct((blk, feat_q), jnp.bfloat16),
        in_specs=[VMEM] * n_col,
        out_specs=VMEM,
        compiler_params=pltpu.CompilerParams(vmem_limit_bytes=8 * 2**20),
        name="combine",
    )(*received)


def solution(mesh):
    return jax.shard_map(
        per_device,
        mesh=mesh,
        in_specs=(P("row", None), P(("row", "col"), None), P(("row", "col"), None)),
        out_specs=P(("row", "col"), None),
        check_vma=False,
    )
```

```python
import functools
import math

import jax
import jax.numpy as jnp
from jax import lax
from jax.experimental import pallas as pl
from jax.experimental.pallas import tpu as pltpu
from jax.sharding import PartitionSpec as P

HEAD = 256
SCALE = 0.0625
CAP = 50.0
LANES = 128
VMEM = pl.BlockSpec(memory_space=pltpu.VMEM)


def turned(mask, n_col):
    half = (n_col.bit_length() - 1) // 2
    return mask >> half | (mask & (1 << half) - 1) << half if 1 << 2 * half == n_col else mask


def stack_blocks(srcs, k_all, v_all, blk):
    first = lax.axis_index("row") % 2 == 0
    for t, src in enumerate(srcs):
        for part, into in (slice(0, blk), k_all), (slice(blk, 2 * blk), v_all):
            value = src[0][part, :]
            if len(src) == 2:
                value = jnp.where(first, value, src[1][part, :])
            into[t * blk : (t + 1) * blk, :] = value


def group_sums(masks, blk, n_col, dests, q_ref, k_all, v_all, emit):
    row, col = lax.axis_index("row"), lax.axis_index("col")
    columns = [col ^ jnp.where(row % 2 == 0, d, turned(d, n_col)) for d in dests]
    kv_heads = k_all.shape[1] // HEAD
    group = q_ref.shape[1] // k_all.shape[1]
    n_keys = len(masks) * blk
    lane = lax.broadcasted_iota(jnp.int32, (1, n_keys), 1)
    key_pos = jnp.zeros((1, n_keys), jnp.int32)
    for t, mask in enumerate(masks):
        start = ((row ^ mask) * n_col + col) * blk
        key_pos = jnp.where(lane // blk == t, start + lane % blk, key_pos)
    sub = lax.broadcasted_iota(jnp.int32, (blk, 1), 0)
    parts = [pl.ds(pl.multiple_of(c * blk, blk), blk) for c in columns]
    pos = jnp.concatenate([(row * n_col + c) * blk + sub for c in columns], axis=0)
    keep = jnp.where(key_pos <= pos, 1.0, 0.0).astype(jnp.float32)
    for kv in range(kv_heads):
        k_head = k_all[:, kv * HEAD : (kv + 1) * HEAD]
        v_head = v_all[:, kv * HEAD : (kv + 1) * HEAD]
        for h in range(kv * group, (kv + 1) * group):
            q_head = jnp.concatenate([q_ref[p, h * HEAD : (h + 1) * HEAD] for p in parts], axis=0)
            scores = lax.dot_general(
                q_head, k_head, (((1,), (1,)), ((), ())), preferred_element_type=jnp.float32
            )
            capped = jnp.tanh(scores * (SCALE / CAP)) * (CAP / math.log(2.0))
            weights = jnp.exp2(capped) * keep
            denom = jnp.sum(weights, axis=1, keepdims=True)
            numer = jnp.dot(
                weights.astype(jnp.bfloat16), v_head, preferred_element_type=jnp.float32
            )
            emit(h, numer, denom)


def chunks_of(n_col):
    size = min(n_col, 4)
    return [range(base, base + size) for base in range(0, n_col, size)]


def sums_kernel(masks, widths, sums_in, last, blk, n_col, q_ref, *refs):
    before, refs = refs[: 2 * sums_in], refs[2 * sums_in :]
    srcs = []
    for width in widths:
        srcs.append(refs[:width])
        refs = refs[width:]
    outs, (k_all, v_all) = refs[:-2], refs[-2:]
    feat_q = q_ref.shape[1]
    stack_blocks(srcs, k_all, v_all, blk)
    for dests in chunks_of(n_col):
        rows = slice(dests[0] * blk, (dests[-1] + 1) * blk)
        lanes = lax.broadcasted_iota(jnp.int32, (len(dests) * blk, LANES), 1)
        total = [before[1][rows, :] if sums_in else jnp.zeros(lanes.shape, jnp.float32)]

        def emit(h, numer, denom, dests=dests, rows=rows, lanes=lanes, total=total):
            cut = slice(h * HEAD, (h + 1) * HEAD)
            if sums_in:
                numer = numer + before[0][rows, cut]
            if last:
                numer = numer.astype(jnp.bfloat16)
                for i, d in enumerate(dests):
                    outs[d][:, cut] = numer[i * blk : (i + 1) * blk]
            else:
                outs[0][rows, cut] = numer
            total[0] = total[0] + jnp.where(lanes % (LANES // 2) == h, denom, 0.0)

        group_sums(masks, blk, n_col, dests, q_ref, k_all, v_all, emit)
        if last:
            high = total[0].astype(jnp.bfloat16).astype(jnp.float32)
            tail = jnp.where(lanes < LANES // 2, high, total[0] - high).astype(jnp.bfloat16)
            for i, d in enumerate(dests):
                outs[d][:, feat_q:] = tail[i * blk : (i + 1) * blk]
        else:
            outs[1][rows, :] = total[0]


def combine_kernel(*refs):
    parts, out_ref = refs[:-1], refs[-1]
    feat_q = out_ref.shape[1]
    tail = sum(p[:, feat_q:].astype(jnp.float32) for p in parts)
    inverse = 1.0 / (tail + pltpu.roll(tail, LANES // 2, 1))
    for h in range(feat_q // HEAD):
        cut = slice(h * HEAD, (h + 1) * HEAD)
        numer = sum(p[:, cut].astype(jnp.float32) for p in parts)
        out_ref[:, cut] = (numer * inverse[:, h : h + 1]).astype(jnp.bfloat16)


def per_device(queries, keys, values):
    blk, feat_k = keys.shape
    span, feat_q = queries.shape
    n_row = lax.axis_size("row")
    n_col = lax.axis_size("col")

    def swap_row(x, mask):
        return lax.ppermute(x, "row", [(i, i ^ mask) for i in range(n_row)])

    def send_up(x, block, hops):
        pairs = []
        for r in range(n_row):
            hop = hops[r % 2]
            if hop is not None and (r ^ hop ^ block) < r ^ hop:
                pairs += [(r * n_col + c, (r ^ hop) * n_col + c) for c in range(n_col)]
        return lax.ppermute(x, ("row", "col"), pairs)

    def swap_col(x, mask):
        masks = [mask, turned(mask, n_col)]
        pairs = [
            (r * n_col + c, r * n_col + (c ^ masks[r % 2])) for r in range(n_row) for c in range(n_col)
        ]
        return lax.ppermute(x, ("row", "col"), pairs)

    def sums(masks, before, last, name):
        message = jax.ShapeDtypeStruct((blk, feat_q + LANES), jnp.bfloat16)
        totals = [
            jax.ShapeDtypeStruct((span, feat_q), jnp.float32),
            jax.ShapeDtypeStruct((span, LANES), jnp.float32),
        ]
        out_shape = [message] * n_col if last else totals
        widths = [len(blocks[m]) for m in masks]
        args = [queries, *before, *[x for m in masks for x in blocks[m]]]
        return pl.pallas_call(
            functools.partial(sums_kernel, masks, widths, len(before) // 2, last, blk, n_col),
            out_shape=out_shape,
            in_specs=[VMEM] * len(args),
            out_specs=[VMEM] * len(out_shape),
            scratch_shapes=[pltpu.VMEM((len(masks) * blk, feat_k), jnp.bfloat16)] * 2,
            compiler_params=pltpu.CompilerParams(vmem_limit_bytes=limit),
            name=name,
        )(*args)

    limit = 16 * 2**20 if span * n_row <= 4096 else 40 * 2**20
    own = jnp.concatenate([keys, values], axis=0)
    blocks = {0: [own], 1: [swap_row(own, 1)]}
    far = sorted(range(2, n_row, 2), key=lambda m: (m & n_row // 2 == 0, m & 2 == 0))
    for mask in far:
        if mask & n_row // 2 and not mask & 2:
            direct = send_up(own, mask, (mask, None))
            relayed = send_up(blocks[mask ^ 2][0], mask, (None, 2))
            blocks[mask] = [direct, relayed]
        else:
            blocks[mask] = [swap_row(own, mask)]
    totals = sums([0, 1], [], False, "own_chip")
    *totals, arrived = lax.optimization_barrier((*totals, [blocks[m] for m in far]))
    blocks.update(zip(far, arrived))
    for mask in far:
        blocks[mask ^ 1] = [swap_row(x, 1) for x in blocks[mask]][::-1]
    totals = sums(far, totals, False, "far_same_core")
    messages = sums([m ^ 1 for m in far], totals, True, "far_other_core")
    received = [messages[0]] + [swap_col(messages[j], j) for j in range(1, n_col)]
    return pl.pallas_call(
        combine_kernel,
        out_shape=jax.ShapeDtypeStruct((blk, feat_q), jnp.bfloat16),
        in_specs=[VMEM] * n_col,
        out_specs=VMEM,
        compiler_params=pltpu.CompilerParams(vmem_limit_bytes=8 * 2**20),
        name="combine",
    )(*received)


def solution(mesh):
    return jax.shard_map(
        per_device,
        mesh=mesh,
        in_specs=(P("row", None), P(("row", "col"), None), P(("row", "col"), None)),
        out_specs=P(("row", "col"), None),
        check_vma=False,
    )
```

```python
import functools
import math

import jax
import jax.numpy as jnp
from jax import lax
from jax.experimental import pallas as pl
from jax.experimental.pallas import tpu as pltpu
from jax.sharding import PartitionSpec as P

HEAD = 256
SCALE = 0.0625
CAP = 50.0
LANES = 128
VMEM = pl.BlockSpec(memory_space=pltpu.VMEM)


def turned(mask, n_col):
    half = (n_col.bit_length() - 1) // 2
    return mask >> half | (mask & (1 << half) - 1) << half if 1 << 2 * half == n_col else mask


def stack_blocks(srcs, k_all, v_all, blk):
    first = lax.axis_index("row") % 2 == 0
    for t, src in enumerate(srcs):
        for part, into in (slice(0, blk), k_all), (slice(blk, 2 * blk), v_all):
            value = src[0][part, :]
            if len(src) == 2:
                value = jnp.where(first, value, src[1][part, :])
            into[t * blk : (t + 1) * blk, :] = value


def group_sums(masks, blk, n_col, dests, q_ref, k_all, v_all, emit):
    row, col = lax.axis_index("row"), lax.axis_index("col")
    columns = [col ^ jnp.where(row % 2 == 0, d, turned(d, n_col)) for d in dests]
    kv_heads = k_all.shape[1] // HEAD
    group = q_ref.shape[1] // k_all.shape[1]
    n_keys = len(masks) * blk
    lane = lax.broadcasted_iota(jnp.int32, (1, n_keys), 1)
    key_pos = jnp.zeros((1, n_keys), jnp.int32)
    for t, mask in enumerate(masks):
        start = ((row ^ mask) * n_col + col) * blk
        key_pos = jnp.where(lane // blk == t, start + lane % blk, key_pos)
    sub = lax.broadcasted_iota(jnp.int32, (blk, 1), 0)
    parts = [pl.ds(pl.multiple_of(c * blk, blk), blk) for c in columns]
    pos = jnp.concatenate([(row * n_col + c) * blk + sub for c in columns], axis=0)
    keep = jnp.where(key_pos <= pos, 1.0, 0.0).astype(jnp.float32)
    for kv in range(kv_heads):
        k_head = k_all[:, kv * HEAD : (kv + 1) * HEAD]
        v_head = v_all[:, kv * HEAD : (kv + 1) * HEAD]
        for h in range(kv * group, (kv + 1) * group):
            q_head = jnp.concatenate([q_ref[p, h * HEAD : (h + 1) * HEAD] for p in parts], axis=0)
            scores = lax.dot_general(
                q_head, k_head, (((1,), (1,)), ((), ())), preferred_element_type=jnp.float32
            )
            capped = jnp.tanh(scores * (SCALE / CAP)) * (CAP / math.log(2.0))
            weights = jnp.exp2(capped) * keep
            denom = jnp.sum(weights, axis=1, keepdims=True)
            numer = jnp.dot(
                weights.astype(jnp.bfloat16), v_head, preferred_element_type=jnp.float32
            )
            emit(h, numer, denom)


def chunks_of(n_col):
    size = min(n_col, 4)
    return [range(base, base + size) for base in range(0, n_col, size)]


def sums_kernel(masks, widths, sums_in, last, blk, n_col, q_ref, *refs):
    before, refs = refs[: 2 * sums_in], refs[2 * sums_in :]
    srcs = []
    for width in widths:
        srcs.append(refs[:width])
        refs = refs[width:]
    outs, (k_all, v_all) = refs[:-2], refs[-2:]
    feat_q = q_ref.shape[1]
    stack_blocks(srcs, k_all, v_all, blk)
    for dests in chunks_of(n_col):
        rows = slice(dests[0] * blk, (dests[-1] + 1) * blk)
        lanes = lax.broadcasted_iota(jnp.int32, (len(dests) * blk, LANES), 1)
        total = [before[1][rows, :] if sums_in else jnp.zeros(lanes.shape, jnp.float32)]

        def emit(h, numer, denom, dests=dests, rows=rows, lanes=lanes, total=total):
            cut = slice(h * HEAD, (h + 1) * HEAD)
            if sums_in:
                numer = numer + before[0][rows, cut]
            if last:
                numer = numer.astype(jnp.bfloat16)
                for i, d in enumerate(dests):
                    outs[d][:, cut] = numer[i * blk : (i + 1) * blk]
            else:
                outs[0][rows, cut] = numer
            total[0] = total[0] + jnp.where(lanes % (LANES // 2) == h, denom, 0.0)

        group_sums(masks, blk, n_col, dests, q_ref, k_all, v_all, emit)
        if last:
            high = total[0].astype(jnp.bfloat16).astype(jnp.float32)
            tail = jnp.where(lanes < LANES // 2, high, total[0] - high).astype(jnp.bfloat16)
            for i, d in enumerate(dests):
                outs[d][:, feat_q:] = tail[i * blk : (i + 1) * blk]
        else:
            outs[1][rows, :] = total[0]


def combine_kernel(*refs):
    parts, out_ref = refs[:-1], refs[-1]
    feat_q = out_ref.shape[1]
    tail = sum(p[:, feat_q:].astype(jnp.float32) for p in parts)
    inverse = 1.0 / (tail + pltpu.roll(tail, LANES // 2, 1))
    for h in range(feat_q // HEAD):
        cut = slice(h * HEAD, (h + 1) * HEAD)
        numer = sum(p[:, cut].astype(jnp.float32) for p in parts)
        out_ref[:, cut] = (numer * inverse[:, h : h + 1]).astype(jnp.bfloat16)


def per_device(queries, keys, values):
    blk, feat_k = keys.shape
    span, feat_q = queries.shape
    n_row = lax.axis_size("row")
    n_col = lax.axis_size("col")

    def swap_row(x, mask):
        return lax.ppermute(x, "row", [(i, i ^ mask) for i in range(n_row)])

    def send_up(x, block, hops):
        pairs = []
        for r in range(n_row):
            hop = hops[r % 2]
            if hop is not None and (r ^ hop ^ block) < r ^ hop:
                pairs += [(r * n_col + c, (r ^ hop) * n_col + c) for c in range(n_col)]
        return lax.ppermute(x, ("row", "col"), pairs)

    def swap_col(x, mask):
        masks = [mask, turned(mask, n_col)]
        pairs = [
            (r * n_col + c, r * n_col + (c ^ masks[r % 2])) for r in range(n_row) for c in range(n_col)
        ]
        return lax.ppermute(x, ("row", "col"), pairs)

    def sums(masks, before, last, name):
        message = jax.ShapeDtypeStruct((blk, feat_q + LANES), jnp.bfloat16)
        totals = [
            jax.ShapeDtypeStruct((span, feat_q), jnp.float32),
            jax.ShapeDtypeStruct((span, LANES), jnp.float32),
        ]
        out_shape = [message] * n_col if last else totals
        widths = [len(blocks[m]) for m in masks]
        args = [queries, *before, *[x for m in masks for x in blocks[m]]]
        return pl.pallas_call(
            functools.partial(sums_kernel, masks, widths, len(before) // 2, last, blk, n_col),
            out_shape=out_shape,
            in_specs=[VMEM] * len(args),
            out_specs=[VMEM] * len(out_shape),
            scratch_shapes=[pltpu.VMEM((len(masks) * blk, feat_k), jnp.bfloat16)] * 2,
            compiler_params=pltpu.CompilerParams(vmem_limit_bytes=limit),
            name=name,
        )(*args)

    limit = 16 * 2**20 if span * n_row <= 4096 else 40 * 2**20
    own = jnp.concatenate([keys, values], axis=0)
    top = n_row // 2
    near = list(range(2, top, 2))
    once = [m for m in range(top, n_row, 2) if m & 2]
    split = [m for m in range(top, n_row, 2) if not m & 2]
    blocks = {0: [own]}
    for mask in once + near:
        blocks[mask] = [swap_row(own, mask)]
    totals = sums([0], [], False, "own_block")
    for mask in split:
        blocks[mask] = [send_up(own, mask, (mask, None))]
    *totals, arrived = lax.optimization_barrier((*totals, [blocks[m] for m in once]))
    blocks.update(zip(once, arrived))
    for mask in split:
        blocks[mask].append(send_up(blocks[mask ^ 2][0], mask, (None, 2)))
    far = split + once + near
    for mask in [0] + far:
        blocks[mask ^ 1] = [swap_row(x, 1) for x in blocks[mask]][::-1]
    totals = sums(far, totals, False, "far_same_core")
    messages = sums([m ^ 1 for m in [0] + far], totals, True, "far_other_core")
    received = [messages[0]] + [swap_col(messages[j], j) for j in range(1, n_col)]
    return pl.pallas_call(
        combine_kernel,
        out_shape=jax.ShapeDtypeStruct((blk, feat_q), jnp.bfloat16),
        in_specs=[VMEM] * n_col,
        out_specs=VMEM,
        compiler_params=pltpu.CompilerParams(vmem_limit_bytes=8 * 2**20),
        name="combine",
    )(*received)


def solution(mesh):
    return jax.shard_map(
        per_device,
        mesh=mesh,
        in_specs=(P("row", None), P(("row", "col"), None), P(("row", "col"), None)),
        out_specs=P(("row", "col"), None),
        check_vma=False,
    )
```

```python
import functools
import math

import jax
import jax.numpy as jnp
from jax import lax
from jax.experimental import pallas as pl
from jax.experimental.pallas import tpu as pltpu
from jax.sharding import PartitionSpec as P

HEAD = 256
SCALE = 0.0625
CAP = 50.0
LANES = 128
VMEM = pl.BlockSpec(memory_space=pltpu.VMEM)


def turned(mask, n_col):
    half = (n_col.bit_length() - 1) // 2
    return mask >> half | (mask & (1 << half) - 1) << half if 1 << 2 * half == n_col else mask


def stack_blocks(srcs, k_all, v_all, blk):
    first = lax.axis_index("row") % 2 == 0
    for t, src in enumerate(srcs):
        for part, into in (slice(0, blk), k_all), (slice(blk, 2 * blk), v_all):
            value = src[0][part, :]
            if len(src) == 2:
                value = jnp.where(first, value, src[1][part, :])
            into[t * blk : (t + 1) * blk, :] = value


def group_sums(masks, blk, n_col, dests, q_ref, k_all, v_all, emit):
    row, col = lax.axis_index("row"), lax.axis_index("col")
    columns = [col ^ jnp.where(row % 2 == 0, d, turned(d, n_col)) for d in dests]
    kv_heads = k_all.shape[1] // HEAD
    group = q_ref.shape[1] // k_all.shape[1]
    n_keys = len(masks) * blk
    lane = lax.broadcasted_iota(jnp.int32, (1, n_keys), 1)
    key_pos = jnp.zeros((1, n_keys), jnp.int32)
    for t, mask in enumerate(masks):
        start = ((row ^ mask) * n_col + col) * blk
        key_pos = jnp.where(lane // blk == t, start + lane % blk, key_pos)
    sub = lax.broadcasted_iota(jnp.int32, (blk, 1), 0)
    parts = [pl.ds(pl.multiple_of(c * blk, blk), blk) for c in columns]
    pos = jnp.concatenate([(row * n_col + c) * blk + sub for c in columns], axis=0)
    keep = jnp.where(key_pos <= pos, 1.0, 0.0).astype(jnp.float32)
    scores = [
        lax.dot_general(
            jnp.concatenate([q_ref[p, h * HEAD : (h + 1) * HEAD] for p in parts], axis=0),
            k_all[:, h // group * HEAD : (h // group + 1) * HEAD],
            (((1,), (1,)), ((), ())),
            preferred_element_type=jnp.float32,
        )
        for h in range(kv_heads * group)
    ]
    weights = []
    for score in scores:
        capped = jnp.tanh(score * (SCALE / CAP)) * (CAP / math.log(2.0))
        weights.append(jnp.exp2(capped) * keep)
    for h, weight in enumerate(weights):
        denom = jnp.sum(weight, axis=1, keepdims=True)
        numer = jnp.dot(
            weight.astype(jnp.bfloat16),
            v_all[:, h // group * HEAD : (h // group + 1) * HEAD],
            preferred_element_type=jnp.float32,
        )
        emit(h, numer, denom)


def chunks_of(n_col):
    size = min(n_col, 4)
    return [range(base, base + size) for base in range(0, n_col, size)]


def sums_kernel(masks, widths, sums_in, last, blk, n_col, q_ref, *refs):
    before, refs = refs[: 2 * sums_in], refs[2 * sums_in :]
    srcs = []
    for width in widths:
        srcs.append(refs[:width])
        refs = refs[width:]
    outs, (k_all, v_all) = refs[:-2], refs[-2:]
    feat_q = q_ref.shape[1]
    stack_blocks(srcs, k_all, v_all, blk)
    for dests in chunks_of(n_col):
        rows = slice(dests[0] * blk, (dests[-1] + 1) * blk)
        lanes = lax.broadcasted_iota(jnp.int32, (len(dests) * blk, LANES), 1)
        total = [before[1][rows, :] if sums_in else jnp.zeros(lanes.shape, jnp.float32)]

        def emit(h, numer, denom, dests=dests, rows=rows, lanes=lanes, total=total):
            cut = slice(h * HEAD, (h + 1) * HEAD)
            if sums_in:
                numer = numer + before[0][rows, cut]
            if last:
                numer = numer.astype(jnp.bfloat16)
                for i, d in enumerate(dests):
                    outs[d][:, cut] = numer[i * blk : (i + 1) * blk]
            else:
                outs[0][rows, cut] = numer
            total[0] = total[0] + jnp.where(lanes % (LANES // 2) == h, denom, 0.0)

        group_sums(masks, blk, n_col, dests, q_ref, k_all, v_all, emit)
        if last:
            high = total[0].astype(jnp.bfloat16).astype(jnp.float32)
            tail = jnp.where(lanes < LANES // 2, high, total[0] - high).astype(jnp.bfloat16)
            for i, d in enumerate(dests):
                outs[d][:, feat_q:] = tail[i * blk : (i + 1) * blk]
        else:
            outs[1][rows, :] = total[0]


def combine_kernel(*refs):
    parts, out_ref = refs[:-1], refs[-1]
    feat_q = out_ref.shape[1]
    tail = sum(p[:, feat_q:].astype(jnp.float32) for p in parts)
    inverse = 1.0 / (tail + pltpu.roll(tail, LANES // 2, 1))
    for h in range(feat_q // HEAD):
        cut = slice(h * HEAD, (h + 1) * HEAD)
        numer = sum(p[:, cut].astype(jnp.float32) for p in parts)
        out_ref[:, cut] = (numer * inverse[:, h : h + 1]).astype(jnp.bfloat16)


def per_device(queries, keys, values):
    blk, feat_k = keys.shape
    span, feat_q = queries.shape
    n_row = lax.axis_size("row")
    n_col = lax.axis_size("col")

    def swap_row(x, mask):
        return lax.ppermute(x, "row", [(i, i ^ mask) for i in range(n_row)])

    def send_up(x, block, hops):
        pairs = []
        for r in range(n_row):
            hop = hops[r % 2]
            if hop is not None and (r ^ hop ^ block) < r ^ hop:
                pairs += [(r * n_col + c, (r ^ hop) * n_col + c) for c in range(n_col)]
        return lax.ppermute(x, ("row", "col"), pairs)

    def swap_col(x, mask):
        masks = [mask, turned(mask, n_col)]
        pairs = [
            (r * n_col + c, r * n_col + (c ^ masks[r % 2])) for r in range(n_row) for c in range(n_col)
        ]
        return lax.ppermute(x, ("row", "col"), pairs)

    def sums(masks, before, last, name):
        message = jax.ShapeDtypeStruct((blk, feat_q + LANES), jnp.bfloat16)
        totals = [
            jax.ShapeDtypeStruct((span, feat_q), jnp.float32),
            jax.ShapeDtypeStruct((span, LANES), jnp.float32),
        ]
        out_shape = [message] * n_col if last else totals
        widths = [len(blocks[m]) for m in masks]
        args = [queries, *before, *[x for m in masks for x in blocks[m]]]
        return pl.pallas_call(
            functools.partial(sums_kernel, masks, widths, len(before) // 2, last, blk, n_col),
            out_shape=out_shape,
            in_specs=[VMEM] * len(args),
            out_specs=[VMEM] * len(out_shape),
            scratch_shapes=[pltpu.VMEM((len(masks) * blk, feat_k), jnp.bfloat16)] * 2,
            compiler_params=pltpu.CompilerParams(vmem_limit_bytes=limit),
            name=name,
        )(*args)

    limit = 16 * 2**20 if span * n_row <= 4096 else 40 * 2**20
    own = jnp.concatenate([keys, values], axis=0)
    top = n_row // 2
    near = list(range(2, top, 2))
    once = [m for m in range(top, n_row, 2) if m & 2]
    split = [m for m in range(top, n_row, 2) if not m & 2]
    blocks = {0: [own]}
    for mask in once + near:
        blocks[mask] = [swap_row(own, mask)]
    totals = sums([0], [], False, "own_block")
    for mask in split:
        blocks[mask] = [send_up(own, mask, (mask, None))]
    *totals, arrived = lax.optimization_barrier((*totals, [blocks[m] for m in once]))
    blocks.update(zip(once, arrived))
    for mask in split:
        blocks[mask].append(send_up(blocks[mask ^ 2][0], mask, (None, 2)))
    far = split + once + near
    for mask in [0] + far:
        blocks[mask ^ 1] = [swap_row(x, 1) for x in blocks[mask]][::-1]
    totals = sums([1] + far, totals, False, "far_same_core")
    messages = sums([m ^ 1 for m in far], totals, True, "far_other_core")
    received = [messages[0]] + [swap_col(messages[j], j) for j in range(1, n_col)]
    return pl.pallas_call(
        combine_kernel,
        out_shape=jax.ShapeDtypeStruct((blk, feat_q), jnp.bfloat16),
        in_specs=[VMEM] * n_col,
        out_specs=VMEM,
        compiler_params=pltpu.CompilerParams(vmem_limit_bytes=8 * 2**20),
        name="combine",
    )(*received)


def solution(mesh):
    return jax.shard_map(
        per_device,
        mesh=mesh,
        in_specs=(P("row", None), P(("row", "col"), None), P(("row", "col"), None)),
        out_specs=P(("row", "col"), None),
        check_vma=False,
    )
```

```python
import functools
import math

import jax
import jax.numpy as jnp
from jax import lax
from jax.experimental import pallas as pl
from jax.experimental.pallas import tpu as pltpu
from jax.sharding import PartitionSpec as P

HEAD = 256
SCALE = 0.0625
CAP = 50.0
LANES = 128
VMEM = pl.BlockSpec(memory_space=pltpu.VMEM)


def turned(mask, n_col):
    half = (n_col.bit_length() - 1) // 2
    return mask >> half | (mask & (1 << half) - 1) << half if 1 << 2 * half == n_col else mask


def stack_blocks(srcs, k_all, v_all, blk):
    first = lax.axis_index("row") % 2 == 0
    for t, src in enumerate(srcs):
        for part, into in (slice(0, blk), k_all), (slice(blk, 2 * blk), v_all):
            value = src[0][part, :]
            if len(src) == 2:
                value = jnp.where(first, value, src[1][part, :])
            into[t * blk : (t + 1) * blk, :] = value


def group_sums(masks, blk, n_col, dests, q_ref, k_all, v_all, emit):
    row, col = lax.axis_index("row"), lax.axis_index("col")
    columns = [col ^ jnp.where(row % 2 == 0, d, turned(d, n_col)) for d in dests]
    kv_heads = k_all.shape[1] // HEAD
    group = q_ref.shape[1] // k_all.shape[1]
    n_keys = len(masks) * blk
    lane = lax.broadcasted_iota(jnp.int32, (1, n_keys), 1)
    key_pos = jnp.zeros((1, n_keys), jnp.int32)
    for t, mask in enumerate(masks):
        start = ((row ^ mask) * n_col + col) * blk
        key_pos = jnp.where(lane // blk == t, start + lane % blk, key_pos)
    sub = lax.broadcasted_iota(jnp.int32, (blk, 1), 0)
    parts = [pl.ds(pl.multiple_of(c * blk, blk), blk) for c in columns]
    pos = jnp.concatenate([(row * n_col + c) * blk + sub for c in columns], axis=0)
    keep = jnp.where(key_pos <= pos, 1.0, 0.0).astype(jnp.float32)
    scores = [
        lax.dot_general(
            jnp.concatenate([q_ref[p, h * HEAD : (h + 1) * HEAD] for p in parts], axis=0),
            k_all[:, h // group * HEAD : (h // group + 1) * HEAD],
            (((1,), (1,)), ((), ())),
            preferred_element_type=jnp.float32,
        )
        for h in range(kv_heads * group)
    ]
    weights = []
    for score in scores:
        capped = jnp.tanh(score * (SCALE / CAP)) * (CAP / math.log(2.0))
        weights.append(jnp.exp2(capped) * keep)
    for h, weight in enumerate(weights):
        denom = jnp.sum(weight, axis=1, keepdims=True)
        numer = jnp.dot(
            weight.astype(jnp.bfloat16),
            v_all[:, h // group * HEAD : (h // group + 1) * HEAD],
            preferred_element_type=jnp.float32,
        )
        emit(h, numer, denom)


def chunks_of(n_col):
    size = min(n_col, 4)
    return [range(base, base + size) for base in range(0, n_col, size)]


def sums_kernel(masks, widths, sums_in, last, blk, n_col, q_ref, *refs):
    before, refs = refs[: 2 * sums_in], refs[2 * sums_in :]
    srcs = []
    for width in widths:
        srcs.append(refs[:width])
        refs = refs[width:]
    outs, (k_all, v_all) = refs[:-2], refs[-2:]
    feat_q = q_ref.shape[1]
    stack_blocks(srcs, k_all, v_all, blk)
    for dests in chunks_of(n_col):
        rows = slice(dests[0] * blk, (dests[-1] + 1) * blk)
        lanes = lax.broadcasted_iota(jnp.int32, (len(dests) * blk, LANES), 1)
        total = [before[1][rows, :] if sums_in else jnp.zeros(lanes.shape, jnp.float32)]

        def emit(h, numer, denom, dests=dests, rows=rows, lanes=lanes, total=total):
            cut = slice(h * HEAD, (h + 1) * HEAD)
            if sums_in:
                numer = numer + before[0][rows, cut]
            if last:
                numer = numer.astype(jnp.bfloat16)
                for i, d in enumerate(dests):
                    for t in range(HEAD // LANES):
                        at = (h * HEAD // LANES + t) * blk
                        outs[d][at : at + blk, :] = numer[
                            i * blk : (i + 1) * blk, t * LANES : (t + 1) * LANES
                        ]
            else:
                outs[0][rows, cut] = numer
            total[0] = total[0] + jnp.where(lanes % (LANES // 2) == h, denom, 0.0)

        group_sums(masks, blk, n_col, dests, q_ref, k_all, v_all, emit)
        if last:
            n_heads = feat_q // HEAD
            high = total[0].astype(jnp.bfloat16).astype(jnp.float32)
            tail = jnp.where(lanes < LANES // 2, high, total[0] - high)
            tail = jnp.where(lanes % (LANES // 2) < n_heads, tail, 0.0)
            for i, d in enumerate(dests):
                packed = jnp.zeros((8, LANES), jnp.float32)
                for k in range(blk // 8):
                    eight = tail[i * blk + k * 8 : i * blk + k * 8 + 8]
                    packed = packed + (pltpu.roll(eight, k * n_heads, 1) if k else eight)
                packed = jnp.concatenate([packed, jnp.zeros_like(packed)], axis=0)
                outs[d][blk * (feat_q // LANES) :, :] = packed.astype(jnp.bfloat16)
        else:
            outs[1][rows, :] = total[0]


def combine_kernel(*refs):
    parts, out_ref = refs[:-1], refs[-1]
    blk, feat_q = out_ref.shape
    n_heads = feat_q // HEAD
    tail = sum(p[blk * (feat_q // LANES) :, :].astype(jnp.float32) for p in parts)[:8]
    inverse = 1.0 / (tail + pltpu.roll(tail, LANES // 2, 1))
    for h in range(n_heads):
        lanes = [k * n_heads + h for k in range(blk // 8)]
        scale = jnp.concatenate(
            [jnp.broadcast_to(inverse[:, at : at + 1], (8, LANES)) for at in lanes], axis=0
        )
        for t in range(h * HEAD // LANES, (h + 1) * HEAD // LANES):
            numer = sum(p[t * blk : (t + 1) * blk, :].astype(jnp.float32) for p in parts)
            out_ref[:, t * LANES : (t + 1) * LANES] = (numer * scale).astype(jnp.bfloat16)


def per_device(queries, keys, values):
    blk, feat_k = keys.shape
    span, feat_q = queries.shape
    n_row = lax.axis_size("row")
    n_col = lax.axis_size("col")

    def swap_row(x, mask):
        return lax.ppermute(x, "row", [(i, i ^ mask) for i in range(n_row)])

    def send_up(x, block, hops):
        pairs = []
        for r in range(n_row):
            hop = hops[r % 2]
            if hop is not None and (r ^ hop ^ block) < r ^ hop:
                pairs += [(r * n_col + c, (r ^ hop) * n_col + c) for c in range(n_col)]
        return lax.ppermute(x, ("row", "col"), pairs)

    def swap_col(x, mask):
        masks = [mask, turned(mask, n_col)]
        pairs = [
            (r * n_col + c, r * n_col + (c ^ masks[r % 2])) for r in range(n_row) for c in range(n_col)
        ]
        return lax.ppermute(x, ("row", "col"), pairs)

    def sums(masks, before, last, name):
        message = jax.ShapeDtypeStruct((blk * (feat_q // LANES) + 16, LANES), jnp.bfloat16)
        totals = [
            jax.ShapeDtypeStruct((span, feat_q), jnp.float32),
            jax.ShapeDtypeStruct((span, LANES), jnp.float32),
        ]
        out_shape = [message] * n_col if last else totals
        widths = [len(blocks[m]) for m in masks]
        args = [queries, *before, *[x for m in masks for x in blocks[m]]]
        return pl.pallas_call(
            functools.partial(sums_kernel, masks, widths, len(before) // 2, last, blk, n_col),
            out_shape=out_shape,
            in_specs=[VMEM] * len(args),
            out_specs=[VMEM] * len(out_shape),
            scratch_shapes=[pltpu.VMEM((len(masks) * blk, feat_k), jnp.bfloat16)] * 2,
            compiler_params=pltpu.CompilerParams(vmem_limit_bytes=limit),
            name=name,
        )(*args)

    limit = 16 * 2**20 if span * n_row <= 4096 else 40 * 2**20
    own = jnp.concatenate([keys, values], axis=0)
    top = n_row // 2
    near = list(range(2, top, 2))
    once = [m for m in range(top, n_row, 2) if m & 2]
    split = [m for m in range(top, n_row, 2) if not m & 2]
    blocks = {0: [own]}
    for mask in once + near:
        blocks[mask] = [swap_row(own, mask)]
    totals = sums([0], [], False, "own_block")
    for mask in split:
        blocks[mask] = [send_up(own, mask, (mask, None))]
    *totals, arrived = lax.optimization_barrier((*totals, [blocks[m] for m in once]))
    blocks.update(zip(once, arrived))
    for mask in split:
        blocks[mask].append(send_up(blocks[mask ^ 2][0], mask, (None, 2)))
    far = split + once + near
    for mask in [0] + far:
        blocks[mask ^ 1] = [swap_row(x, 1) for x in blocks[mask]][::-1]
    totals = sums([1] + far, totals, False, "far_same_core")
    messages = sums([m ^ 1 for m in far], totals, True, "far_other_core")
    received = [messages[0]] + [swap_col(messages[j], j) for j in range(1, n_col)]
    return pl.pallas_call(
        combine_kernel,
        out_shape=jax.ShapeDtypeStruct((blk, feat_q), jnp.bfloat16),
        in_specs=[VMEM] * n_col,
        out_specs=VMEM,
        compiler_params=pltpu.CompilerParams(vmem_limit_bytes=8 * 2**20),
        name="combine",
    )(*received)


def solution(mesh):
    return jax.shard_map(
        per_device,
        mesh=mesh,
        in_specs=(P("row", None), P(("row", "col"), None), P(("row", "col"), None)),
        out_specs=P(("row", "col"), None),
        check_vma=False,
    )
```

```python
import functools
import math

import jax
import jax.numpy as jnp
from jax import lax
from jax.experimental import pallas as pl
from jax.experimental.pallas import tpu as pltpu
from jax.sharding import PartitionSpec as P

HEAD = 256
SCALE = 0.0625
CAP = 50.0
LANES = 128
VMEM = pl.BlockSpec(memory_space=pltpu.VMEM)


def turned(mask, n_col):
    half = (n_col.bit_length() - 1) // 2
    return mask >> half | (mask & (1 << half) - 1) << half if 1 << 2 * half == n_col else mask


def stack_blocks(srcs, k_all, v_all, blk):
    first = lax.axis_index("row") % 2 == 0
    for t, src in enumerate(srcs):
        for part, into in (slice(0, blk), k_all), (slice(blk, 2 * blk), v_all):
            value = src[0][part, :]
            if len(src) == 2:
                value = jnp.where(first, value, src[1][part, :])
            into[t * blk : (t + 1) * blk, :] = value


def group_sums(masks, blk, n_col, dests, q_ref, k_all, v_all, emit):
    row, col = lax.axis_index("row"), lax.axis_index("col")
    columns = [col ^ jnp.where(row % 2 == 0, d, turned(d, n_col)) for d in dests]
    kv_heads = k_all.shape[1] // HEAD
    group = q_ref.shape[1] // k_all.shape[1]
    n_keys = len(masks) * blk
    lane = lax.broadcasted_iota(jnp.int32, (1, n_keys), 1)
    key_pos = jnp.zeros((1, n_keys), jnp.int32)
    for t, mask in enumerate(masks):
        start = ((row ^ mask) * n_col + col) * blk
        key_pos = jnp.where(lane // blk == t, start + lane % blk, key_pos)
    sub = lax.broadcasted_iota(jnp.int32, (blk, 1), 0)
    parts = [pl.ds(pl.multiple_of(c * blk, blk), blk) for c in columns]
    pos = jnp.concatenate([(row * n_col + c) * blk + sub for c in columns], axis=0)
    keep = jnp.where(key_pos <= pos, 1.0, 0.0).astype(jnp.float32)
    scores = [
        lax.dot_general(
            jnp.concatenate([q_ref[p, h * HEAD : (h + 1) * HEAD] for p in parts], axis=0),
            k_all[:, h // group * HEAD : (h // group + 1) * HEAD],
            (((1,), (1,)), ((), ())),
            preferred_element_type=jnp.float32,
        )
        for h in range(kv_heads * group)
    ]
    weights = []
    for score in scores:
        capped = jnp.tanh(score * (SCALE / CAP)) * (CAP / math.log(2.0))
        weights.append(jnp.exp2(capped) * keep)
    for h, weight in enumerate(weights):
        denom = jnp.sum(weight, axis=1, keepdims=True)
        numer = jnp.dot(
            weight.astype(jnp.bfloat16),
            v_all[:, h // group * HEAD : (h // group + 1) * HEAD],
            preferred_element_type=jnp.float32,
        )
        emit(h, numer, denom)


def chunks_of(n_col):
    size = min(n_col, 4)
    return [range(base, base + size) for base in range(0, n_col, size)]


def sums_kernel(masks, widths, sums_in, last, blk, n_col, q_ref, *refs):
    before, refs = refs[: 2 * sums_in], refs[2 * sums_in :]
    srcs = []
    for width in widths:
        srcs.append(refs[:width])
        refs = refs[width:]
    outs, (k_all, v_all) = refs[:-2], refs[-2:]
    feat_q = q_ref.shape[1]
    stack_blocks(srcs, k_all, v_all, blk)
    for dests in chunks_of(n_col):
        rows = slice(dests[0] * blk, (dests[-1] + 1) * blk)
        lanes = lax.broadcasted_iota(jnp.int32, (len(dests) * blk, LANES), 1)
        total = [before[1][rows, :] if sums_in else jnp.zeros(lanes.shape, jnp.float32)]

        def emit(h, numer, denom, dests=dests, rows=rows, lanes=lanes, total=total):
            cut = slice(h * HEAD, (h + 1) * HEAD)
            if sums_in:
                numer = numer + before[0][rows, cut]
            if last:
                numer = numer.astype(jnp.bfloat16)
                for i, d in enumerate(dests):
                    for t in range(HEAD // LANES):
                        at = (h * HEAD // LANES + t) * blk
                        outs[d][at : at + blk, :] = numer[
                            i * blk : (i + 1) * blk, t * LANES : (t + 1) * LANES
                        ]
            else:
                outs[0][rows, cut] = numer
            total[0] = total[0] + jnp.where(lanes % (LANES // 2) == h, denom, 0.0)

        group_sums(masks, blk, n_col, dests, q_ref, k_all, v_all, emit)
        if last:
            n_heads = feat_q // HEAD
            high = total[0].astype(jnp.bfloat16).astype(jnp.float32)
            tail = jnp.where(lanes < LANES // 2, high, total[0] - high)
            tail = jnp.where(lanes % (LANES // 2) < n_heads, tail, 0.0)
            for i, d in enumerate(dests):
                packed = jnp.zeros((8, LANES), jnp.float32)
                for k in range(blk // 8):
                    eight = tail[i * blk + k * 8 : i * blk + k * 8 + 8]
                    packed = packed + (pltpu.roll(eight, k * n_heads, 1) if k else eight)
                packed = jnp.concatenate([packed, jnp.zeros_like(packed)], axis=0)
                outs[d][blk * (feat_q // LANES) :, :] = packed.astype(jnp.bfloat16)
        else:
            outs[1][rows, :] = total[0]


def combine_kernel(*refs):
    parts, out_ref = refs[:-1], refs[-1]
    blk, feat_q = out_ref.shape
    n_heads = feat_q // HEAD
    tail = sum(p[blk * (feat_q // LANES) :, :].astype(jnp.float32) for p in parts)[:8]
    inverse = 1.0 / (tail + pltpu.roll(tail, LANES // 2, 1))
    for h in range(n_heads):
        lanes = [k * n_heads + h for k in range(blk // 8)]
        scale = jnp.concatenate(
            [jnp.broadcast_to(inverse[:, at : at + 1], (8, LANES)) for at in lanes], axis=0
        )
        for t in range(h * HEAD // LANES, (h + 1) * HEAD // LANES):
            numer = sum(p[t * blk : (t + 1) * blk, :].astype(jnp.float32) for p in parts)
            out_ref[:, t * LANES : (t + 1) * LANES] = (numer * scale).astype(jnp.bfloat16)


def per_device(queries, keys, values):
    blk, feat_k = keys.shape
    span, feat_q = queries.shape
    n_row = lax.axis_size("row")
    n_col = lax.axis_size("col")

    def swap_row(x, mask):
        return lax.ppermute(x, "row", [(i, i ^ mask) for i in range(n_row)])

    def send_up(x, block, hops):
        pairs = []
        for r in range(n_row):
            hop = hops[r % 2]
            if hop is not None and (r ^ hop ^ block) < r ^ hop:
                pairs += [(r * n_col + c, (r ^ hop) * n_col + c) for c in range(n_col)]
        return lax.ppermute(x, ("row", "col"), pairs)

    def swap_col(x, mask):
        masks = [mask, turned(mask, n_col)]
        pairs = [
            (r * n_col + c, r * n_col + (c ^ masks[r % 2])) for r in range(n_row) for c in range(n_col)
        ]
        return lax.ppermute(x, ("row", "col"), pairs)

    def sums(masks, before, last, name):
        message = jax.ShapeDtypeStruct((blk * (feat_q // LANES) + 16, LANES), jnp.bfloat16)
        totals = [
            jax.ShapeDtypeStruct((span, feat_q), jnp.float32),
            jax.ShapeDtypeStruct((span, LANES), jnp.float32),
        ]
        out_shape = [message] * n_col if last else totals
        widths = [len(blocks[m]) for m in masks]
        args = [queries, *before, *[x for m in masks for x in blocks[m]]]
        return pl.pallas_call(
            functools.partial(sums_kernel, masks, widths, len(before) // 2, last, blk, n_col),
            out_shape=out_shape,
            in_specs=[VMEM] * len(args),
            out_specs=[VMEM] * len(out_shape),
            scratch_shapes=[pltpu.VMEM((len(masks) * blk, feat_k), jnp.bfloat16)] * 2,
            compiler_params=pltpu.CompilerParams(vmem_limit_bytes=limit),
            name=name,
        )(*args)

    limit = 16 * 2**20 if span * n_row <= 4096 else 40 * 2**20
    own = jnp.concatenate([keys, values], axis=0)
    top = n_row // 2
    near = list(range(2, top, 2))
    once = [m for m in range(top, n_row, 2) if m & 2]
    split = [m for m in range(top, n_row, 2) if not m & 2]
    blocks = {0: [own]}
    for mask in once + near:
        blocks[mask] = [swap_row(own, mask)]
    totals = sums([0], [], False, "own_block")
    for mask in split:
        blocks[mask] = [send_up(own, mask, (mask, None))]
    *totals, arrived = lax.optimization_barrier((*totals, [blocks[m] for m in once]))
    blocks.update(zip(once, arrived))
    for mask in split:
        blocks[mask].append(send_up(blocks[mask ^ 2][0], mask, (None, 2)))
    far = near + split + once
    for mask in [0] + far:
        blocks[mask ^ 1] = [swap_row(x, 1) for x in blocks[mask]][::-1]
    totals = sums([1] + far, totals, False, "far_same_core")
    messages = sums([m ^ 1 for m in far], totals, True, "far_other_core")
    received = [messages[0]] + [swap_col(messages[j], j) for j in range(1, n_col)]
    return pl.pallas_call(
        combine_kernel,
        out_shape=jax.ShapeDtypeStruct((blk, feat_q), jnp.bfloat16),
        in_specs=[VMEM] * n_col,
        out_specs=VMEM,
        compiler_params=pltpu.CompilerParams(vmem_limit_bytes=8 * 2**20),
        name="combine",
    )(*received)


def solution(mesh):
    return jax.shard_map(
        per_device,
        mesh=mesh,
        in_specs=(P("row", None), P(("row", "col"), None), P(("row", "col"), None)),
        out_specs=P(("row", "col"), None),
        check_vma=False,
    )
```

```python
import functools
import math

import jax
import jax.numpy as jnp
from jax import lax
from jax.experimental import pallas as pl
from jax.experimental.pallas import tpu as pltpu
from jax.sharding import PartitionSpec as P

HEAD = 256
SCALE = 0.0625
CAP = 50.0
LANES = 128
VMEM = pl.BlockSpec(memory_space=pltpu.VMEM)


def turned(mask, n_col):
    half = (n_col.bit_length() - 1) // 2
    return mask >> half | (mask & (1 << half) - 1) << half if 1 << 2 * half == n_col else mask


def stack_blocks(srcs, k_all, v_all, blk):
    first = lax.axis_index("row") % 2 == 0
    for t, src in enumerate(srcs):
        for part, into in (slice(0, blk), k_all), (slice(blk, 2 * blk), v_all):
            value = src[0][part, :]
            if len(src) == 2:
                value = jnp.where(first, value, src[1][part, :])
            into[t * blk : (t + 1) * blk, :] = value


def group_sums(masks, blk, n_col, dests, q_ref, k_all, v_all, emit):
    row, col = lax.axis_index("row"), lax.axis_index("col")
    columns = [col ^ jnp.where(row % 2 == 0, d, turned(d, n_col)) for d in dests]
    kv_heads = k_all.shape[1] // HEAD
    group = q_ref.shape[1] // k_all.shape[1]
    n_keys = len(masks) * blk
    lane = lax.broadcasted_iota(jnp.int32, (1, n_keys), 1)
    key_pos = jnp.zeros((1, n_keys), jnp.int32)
    for t, mask in enumerate(masks):
        start = ((row ^ mask) * n_col + col) * blk
        key_pos = jnp.where(lane // blk == t, start + lane % blk, key_pos)
    sub = lax.broadcasted_iota(jnp.int32, (blk, 1), 0)
    parts = [pl.ds(pl.multiple_of(c * blk, blk), blk) for c in columns]
    pos = jnp.concatenate([(row * n_col + c) * blk + sub for c in columns], axis=0)
    keep = jnp.where(key_pos <= pos, 1.0, 0.0).astype(jnp.float32)
    scores = [
        lax.dot_general(
            jnp.concatenate([q_ref[p, h * HEAD : (h + 1) * HEAD] for p in parts], axis=0),
            k_all[:, h // group * HEAD : (h // group + 1) * HEAD],
            (((1,), (1,)), ((), ())),
            preferred_element_type=jnp.float32,
        )
        for h in range(kv_heads * group)
    ]
    weights = []
    for score in scores:
        capped = jnp.tanh(score * (SCALE / CAP)) * (CAP / math.log(2.0))
        weights.append(jnp.exp2(capped) * keep)
    for h, weight in enumerate(weights):
        denom = jnp.sum(weight, axis=1, keepdims=True)
        numer = jnp.dot(
            weight.astype(jnp.bfloat16),
            v_all[:, h // group * HEAD : (h // group + 1) * HEAD],
            preferred_element_type=jnp.float32,
        )
        emit(h, numer, denom)


def chunks_of(n_col):
    size = min(n_col, 4)
    return [range(base, base + size) for base in range(0, n_col, size)]


def sums_kernel(masks, widths, sums_in, last, blk, n_col, q_ref, *refs):
    before, refs = refs[: 2 * sums_in], refs[2 * sums_in :]
    srcs = []
    for width in widths:
        srcs.append(refs[:width])
        refs = refs[width:]
    outs, (k_all, v_all) = refs[:-2], refs[-2:]
    feat_q = q_ref.shape[1]
    stack_blocks(srcs, k_all, v_all, blk)
    for dests in chunks_of(n_col):
        rows = slice(dests[0] * blk, (dests[-1] + 1) * blk)
        lanes = lax.broadcasted_iota(jnp.int32, (len(dests) * blk, LANES), 1)
        total = [before[1][rows, :] if sums_in else jnp.zeros(lanes.shape, jnp.float32)]

        def emit(h, numer, denom, dests=dests, rows=rows, lanes=lanes, total=total):
            cut = slice(h * HEAD, (h + 1) * HEAD)
            if sums_in:
                numer = numer + before[0][rows, cut]
            if last:
                numer = numer.astype(jnp.bfloat16)
                for i, d in enumerate(dests):
                    for t in range(HEAD // LANES):
                        at = (h * HEAD // LANES + t) * blk
                        outs[d][at : at + blk, :] = numer[
                            i * blk : (i + 1) * blk, t * LANES : (t + 1) * LANES
                        ]
            else:
                outs[0][rows, cut] = numer
            total[0] = total[0] + jnp.where(lanes % (LANES // 2) == h, denom, 0.0)

        group_sums(masks, blk, n_col, dests, q_ref, k_all, v_all, emit)
        if last:
            n_heads = feat_q // HEAD
            high = total[0].astype(jnp.bfloat16).astype(jnp.float32)
            tail = jnp.where(lanes < LANES // 2, high, total[0] - high)
            tail = jnp.where(lanes % (LANES // 2) < n_heads, tail, 0.0)
            for i, d in enumerate(dests):
                packed = jnp.zeros((8, LANES), jnp.float32)
                for k in range(blk // 8):
                    eight = tail[i * blk + k * 8 : i * blk + k * 8 + 8]
                    packed = packed + (pltpu.roll(eight, k * n_heads, 1) if k else eight)
                packed = jnp.concatenate([packed, jnp.zeros_like(packed)], axis=0)
                outs[d][blk * (feat_q // LANES) :, :] = packed.astype(jnp.bfloat16)
        else:
            outs[1][rows, :] = total[0]


def combine_kernel(*refs):
    parts, out_ref = refs[:-1], refs[-1]
    blk, feat_q = out_ref.shape
    n_heads = feat_q // HEAD
    tail = sum(p[blk * (feat_q // LANES) :, :].astype(jnp.float32) for p in parts)[:8]
    inverse = 1.0 / (tail + pltpu.roll(tail, LANES // 2, 1))
    for h in range(n_heads):
        lanes = [k * n_heads + h for k in range(blk // 8)]
        scale = jnp.concatenate(
            [jnp.broadcast_to(inverse[:, at : at + 1], (8, LANES)) for at in lanes], axis=0
        )
        for t in range(h * HEAD // LANES, (h + 1) * HEAD // LANES):
            numer = sum(p[t * blk : (t + 1) * blk, :].astype(jnp.float32) for p in parts)
            out_ref[:, t * LANES : (t + 1) * LANES] = (numer * scale).astype(jnp.bfloat16)


def per_device(queries, keys, values):
    blk, feat_k = keys.shape
    span, feat_q = queries.shape
    n_row = lax.axis_size("row")
    n_col = lax.axis_size("col")

    def swap_row(x, mask):
        return lax.ppermute(x, "row", [(i, i ^ mask) for i in range(n_row)])

    def send_up(x, block, hops):
        pairs = []
        for r in range(n_row):
            hop = hops[r % 2]
            if hop is not None and (r ^ hop ^ block) < r ^ hop:
                pairs += [(r * n_col + c, (r ^ hop) * n_col + c) for c in range(n_col)]
        return lax.ppermute(x, ("row", "col"), pairs)

    def swap_col(x, mask):
        masks = [mask, turned(mask, n_col)]
        pairs = [
            (r * n_col + c, r * n_col + (c ^ masks[r % 2])) for r in range(n_row) for c in range(n_col)
        ]
        return lax.ppermute(x, ("row", "col"), pairs)

    def sums(masks, before, last, name):
        message = jax.ShapeDtypeStruct((blk * (feat_q // LANES) + 16, LANES), jnp.bfloat16)
        totals = [
            jax.ShapeDtypeStruct((span, feat_q), jnp.float32),
            jax.ShapeDtypeStruct((span, LANES), jnp.float32),
        ]
        out_shape = [message] * n_col if last else totals
        widths = [len(blocks[m]) for m in masks]
        args = [queries, *before, *[x for m in masks for x in blocks[m]]]
        return pl.pallas_call(
            functools.partial(sums_kernel, masks, widths, len(before) // 2, last, blk, n_col),
            out_shape=out_shape,
            in_specs=[VMEM] * len(args),
            out_specs=[VMEM] * len(out_shape),
            scratch_shapes=[pltpu.VMEM((len(masks) * blk, feat_k), jnp.bfloat16)] * 2,
            compiler_params=pltpu.CompilerParams(vmem_limit_bytes=limit),
            name=name,
        )(*args)

    limit = 16 * 2**20 if span * n_row <= 4096 else 40 * 2**20
    own = jnp.concatenate([keys, values], axis=0)
    top = n_row // 2
    near = list(range(2, top, 2))
    once = [m for m in range(top, n_row, 2) if m & 2]
    split = [m for m in range(top, n_row, 2) if not m & 2]
    blocks = {0: [own]}
    for mask in once + near:
        blocks[mask] = [swap_row(own, mask)]
    totals = sums([0], [], False, "own_block")
    for mask in split:
        blocks[mask] = [send_up(own, mask, (mask, None))]
    *totals, arrived = lax.optimization_barrier((*totals, [blocks[m] for m in once]))
    blocks.update(zip(once, arrived))
    for mask in split:
        blocks[mask].append(send_up(blocks[mask ^ 2][0], mask, (None, 2)))
    far = near + split + once
    for mask in [0] + far:
        blocks[mask ^ 1] = [swap_row(x, 1) for x in blocks[mask]][::-1]
    totals = sums([1] + far + [m ^ 1 for m in once], totals, False, "all_but_last")
    messages = sums([m ^ 1 for m in split + near], totals, True, "last")
    received = [messages[0]] + [swap_col(messages[j], j) for j in range(1, n_col)]
    return pl.pallas_call(
        combine_kernel,
        out_shape=jax.ShapeDtypeStruct((blk, feat_q), jnp.bfloat16),
        in_specs=[VMEM] * n_col,
        out_specs=VMEM,
        compiler_params=pltpu.CompilerParams(vmem_limit_bytes=8 * 2**20),
        name="combine",
    )(*received)


def solution(mesh):
    return jax.shard_map(
        per_device,
        mesh=mesh,
        in_specs=(P("row", None), P(("row", "col"), None), P(("row", "col"), None)),
        out_specs=P(("row", "col"), None),
        check_vma=False,
    )
```

```python
import functools
import math

import jax
import jax.numpy as jnp
from jax import lax
from jax.experimental import pallas as pl
from jax.experimental.pallas import tpu as pltpu
from jax.sharding import PartitionSpec as P

HEAD = 256
SCALE = 0.0625
CAP = 50.0
LANES = 128
VMEM = pl.BlockSpec(memory_space=pltpu.VMEM)


def turned(mask, n_col):
    half = (n_col.bit_length() - 1) // 2
    return mask >> half | (mask & (1 << half) - 1) << half if 1 << 2 * half == n_col else mask


def stack_blocks(srcs, k_all, v_all, blk):
    first = lax.axis_index("row") % 2 == 0
    for t, src in enumerate(srcs):
        for part, into in (slice(0, blk), k_all), (slice(blk, 2 * blk), v_all):
            value = src[0][part, :]
            if len(src) == 2:
                value = jnp.where(first, value, src[1][part, :])
            into[t * blk : (t + 1) * blk, :] = value


def group_sums(masks, blk, n_col, dests, q_ref, k_all, v_all, emit):
    row, col = lax.axis_index("row"), lax.axis_index("col")
    columns = [col ^ jnp.where(row % 2 == 0, d, turned(d, n_col)) for d in dests]
    kv_heads = k_all.shape[1] // HEAD
    group = q_ref.shape[1] // k_all.shape[1]
    n_keys = len(masks) * blk
    lane = lax.broadcasted_iota(jnp.int32, (1, n_keys), 1)
    key_pos = jnp.zeros((1, n_keys), jnp.int32)
    for t, mask in enumerate(masks):
        start = ((row ^ mask) * n_col + col) * blk
        key_pos = jnp.where(lane // blk == t, start + lane % blk, key_pos)
    sub = lax.broadcasted_iota(jnp.int32, (blk, 1), 0)
    parts = [pl.ds(pl.multiple_of(c * blk, blk), blk) for c in columns]
    pos = jnp.concatenate([(row * n_col + c) * blk + sub for c in columns], axis=0)
    keep = jnp.where(key_pos <= pos, 1.0, 0.0).astype(jnp.float32)
    scores = [
        lax.dot_general(
            jnp.concatenate([q_ref[p, h * HEAD : (h + 1) * HEAD] for p in parts], axis=0),
            k_all[:, h // group * HEAD : (h // group + 1) * HEAD],
            (((1,), (1,)), ((), ())),
            preferred_element_type=jnp.float32,
        )
        for h in range(kv_heads * group)
    ]
    weights = []
    for score in scores:
        capped = jnp.tanh(score * (SCALE / CAP)) * (CAP / math.log(2.0))
        weights.append(jnp.exp2(capped) * keep)
    for h, weight in enumerate(weights):
        denom = jnp.sum(weight, axis=1, keepdims=True)
        numer = jnp.dot(
            weight.astype(jnp.bfloat16),
            v_all[:, h // group * HEAD : (h // group + 1) * HEAD],
            preferred_element_type=jnp.float32,
        )
        emit(h, numer, denom)


def chunks_of(n_col):
    size = min(n_col, 4)
    return [range(base, base + size) for base in range(0, n_col, size)]


def sums_kernel(masks, widths, sums_in, last, blk, n_col, q_ref, *refs):
    before, refs = refs[: 2 * sums_in], refs[2 * sums_in :]
    srcs = []
    for width in widths:
        srcs.append(refs[:width])
        refs = refs[width:]
    outs, (k_all, v_all) = refs[:-2], refs[-2:]
    feat_q = q_ref.shape[1]
    stack_blocks(srcs, k_all, v_all, blk)
    for dests in chunks_of(n_col):
        rows = slice(dests[0] * blk, (dests[-1] + 1) * blk)
        lanes = lax.broadcasted_iota(jnp.int32, (len(dests) * blk, LANES), 1)
        total = [before[1][rows, :] if sums_in else jnp.zeros(lanes.shape, jnp.float32)]

        def emit(h, numer, denom, dests=dests, rows=rows, lanes=lanes, total=total):
            cut = slice(h * HEAD, (h + 1) * HEAD)
            if sums_in:
                numer = numer + before[0][rows, cut]
            if last:
                numer = numer.astype(jnp.bfloat16)
                for i, d in enumerate(dests):
                    for t in range(HEAD // LANES):
                        at = (h * HEAD // LANES + t) * blk
                        outs[d][at : at + blk, :] = numer[
                            i * blk : (i + 1) * blk, t * LANES : (t + 1) * LANES
                        ]
            else:
                outs[0][rows, cut] = numer
            total[0] = total[0] + jnp.where(lanes % (LANES // 2) == h, denom, 0.0)

        group_sums(masks, blk, n_col, dests, q_ref, k_all, v_all, emit)
        if last:
            n_heads = feat_q // HEAD
            high = total[0].astype(jnp.bfloat16).astype(jnp.float32)
            tail = jnp.where(lanes < LANES // 2, high, total[0] - high)
            tail = jnp.where(lanes % (LANES // 2) < n_heads, tail, 0.0)
            for i, d in enumerate(dests):
                packed = jnp.zeros((8, LANES), jnp.float32)
                for k in range(blk // 8):
                    eight = tail[i * blk + k * 8 : i * blk + k * 8 + 8]
                    packed = packed + (pltpu.roll(eight, k * n_heads, 1) if k else eight)
                packed = jnp.concatenate([packed, jnp.zeros_like(packed)], axis=0)
                outs[d][blk * (feat_q // LANES) :, :] = packed.astype(jnp.bfloat16)
        else:
            outs[1][rows, :] = total[0]


def combine_kernel(*refs):
    parts, out_ref = refs[:-1], refs[-1]
    blk, feat_q = out_ref.shape
    n_heads = feat_q // HEAD
    tail = sum(p[blk * (feat_q // LANES) :, :].astype(jnp.float32) for p in parts)[:8]
    inverse = 1.0 / (tail + pltpu.roll(tail, LANES // 2, 1))
    for h in range(n_heads):
        lanes = [k * n_heads + h for k in range(blk // 8)]
        scale = jnp.concatenate(
            [jnp.broadcast_to(inverse[:, at : at + 1], (8, LANES)) for at in lanes], axis=0
        )
        for t in range(h * HEAD // LANES, (h + 1) * HEAD // LANES):
            numer = sum(p[t * blk : (t + 1) * blk, :].astype(jnp.float32) for p in parts)
            out_ref[:, t * LANES : (t + 1) * LANES] = (numer * scale).astype(jnp.bfloat16)


def per_device(queries, keys, values):
    blk, feat_k = keys.shape
    span, feat_q = queries.shape
    n_row = lax.axis_size("row")
    n_col = lax.axis_size("col")

    def swap_row(x, mask):
        return lax.ppermute(x, "row", [(i, i ^ mask) for i in range(n_row)])

    def send_up(x, block, hops):
        pairs = []
        for r in range(n_row):
            hop = hops[r % 2]
            if hop is not None and (r ^ hop ^ block) < r ^ hop:
                pairs += [(r * n_col + c, (r ^ hop) * n_col + c) for c in range(n_col)]
        return lax.ppermute(x, ("row", "col"), pairs)

    def swap_col(x, mask):
        masks = [mask, turned(mask, n_col)]
        pairs = [
            (r * n_col + c, r * n_col + (c ^ masks[r % 2])) for r in range(n_row) for c in range(n_col)
        ]
        return lax.ppermute(x, ("row", "col"), pairs)

    def sums(masks, before, last, name):
        message = jax.ShapeDtypeStruct((blk * (feat_q // LANES) + 16, LANES), jnp.bfloat16)
        totals = [
            jax.ShapeDtypeStruct((span, feat_q), jnp.float32),
            jax.ShapeDtypeStruct((span, LANES), jnp.float32),
        ]
        out_shape = [message] * n_col if last else totals
        widths = [len(blocks[m]) for m in masks]
        args = [queries, *before, *[x for m in masks for x in blocks[m]]]
        return pl.pallas_call(
            functools.partial(sums_kernel, masks, widths, len(before) // 2, last, blk, n_col),
            out_shape=out_shape,
            in_specs=[VMEM] * len(args),
            out_specs=[VMEM] * len(out_shape),
            scratch_shapes=[pltpu.VMEM((len(masks) * blk, feat_k), jnp.bfloat16)] * 2,
            compiler_params=pltpu.CompilerParams(vmem_limit_bytes=limit),
            name=name,
        )(*args)

    limit = 16 * 2**20 if span * n_row <= 4096 else 40 * 2**20
    own = jnp.concatenate([keys, values], axis=0)
    top = n_row // 2
    near = list(range(2, top, 2))
    once = [m for m in range(top, n_row, 2) if m & 2]
    split = [m for m in range(top, n_row, 2) if not m & 2]
    blocks = {0: [own]}
    partner = swap_row(own, 1)
    for mask in once + near:
        blocks[mask] = [swap_row(own, mask)]
    totals = sums([0], [], False, "own_block")
    for mask in split:
        blocks[mask] = [send_up(own, mask, (mask, None))]
    *totals, arrived = lax.optimization_barrier((*totals, [blocks[m] for m in once]))
    blocks.update(zip(once, arrived))
    for mask in split:
        blocks[mask].append(send_up(blocks[mask ^ 2][0], mask, (None, 2)))
    far = split + once + near
    blocks[1] = [partner]
    for mask in far:
        blocks[mask ^ 1] = [swap_row(x, 1) for x in blocks[mask]][::-1]
    totals = sums([1] + far, totals, False, "far_same_core")
    messages = sums([m ^ 1 for m in far], totals, True, "far_other_core")
    received = [messages[0]] + [swap_col(messages[j], j) for j in range(1, n_col)]
    return pl.pallas_call(
        combine_kernel,
        out_shape=jax.ShapeDtypeStruct((blk, feat_q), jnp.bfloat16),
        in_specs=[VMEM] * n_col,
        out_specs=VMEM,
        compiler_params=pltpu.CompilerParams(vmem_limit_bytes=8 * 2**20),
        name="combine",
    )(*received)


def solution(mesh):
    return jax.shard_map(
        per_device,
        mesh=mesh,
        in_specs=(P("row", None), P(("row", "col"), None), P(("row", "col"), None)),
        out_specs=P(("row", "col"), None),
        check_vma=False,
    )
```
